32 devices in a mesh: occ: 8 (over y, x, core), vir: 4 (over z).
Axes of the slice: x: 2, y: 2, z: 4, core: 2. Of those that a mesh axis runs over, the one named last changes fastest.
Arguments:
- three_index: bfloat16 [2048, 128, 640], P(('occ', 'vir')), may hold values from -0.69921875 to 0.69921875
- virt_coeff: bfloat16 [640, 512], replicated, may hold values from -0.25 to 0.25
- metric_root: bfloat16 [2048, 2048], P(('occ', 'vir')), may hold values from -0.125 to 0.125
- owner_table: int32 [128], replicated, may hold values from 0 to 127, each once
- pair_order: int32 [4], replicated, may hold values from 0 to 7
- occ_energy: float32 [128], replicated, may hold values from -1.5 to -0.3
- vir_energy: float32 [512], replicated, may hold values from 0.1 to 2.5
Outputs:
- density: float32 [128, 512, 2048], P('occ', 'vir')
The draws below stay inside these ranges and needn't reach their ends.
Inputs may be any that keep to these rules, and one draw needn't show every extreme that they name: `owner_table`: each orbital once.
All inputs are finite; a program needn't handle non-finite values.
Results may differ from the reference program's by a relative error of at most 0.0045.
Values may be sent and summed in bfloat16 or wider, within the bound.
A program may use at most 192 MiB of HBM per device.

```python
import jax
import jax.numpy as jnp
from jax import lax

NO = 128
NB = 640
NV = 512
NAUX = 2048
NSTEP = 4
N_OCC = 8
N_VIR = 4


def touch_ends(array, own_key, smallest, high):
    longest = array.shape.index(max(array.shape))
    spots = []
    for shift in (0, 1):
        where = [jax.random.randint(jax.random.fold_in(own_key, axis), (), 0, length) for axis, length in enumerate(array.shape)]
        where[longest] = (where[longest] + shift) % array.shape[longest]
        spots.append(tuple(where))
    return array.at[spots[0]].set(smallest).at[spots[1]].set(high)


def block_levels(own_key, shape, cuts, low, top_value):
    factor_of, own = 1.0, jax.random.fold_in(own_key, 6)
    for position, parts in cuts:
        heights = jnp.exp(jax.random.uniform(jax.random.fold_in(own, position), (parts,), jnp.float32, low / len(cuts), top_value / len(cuts)))
        factor_of = factor_of * jnp.repeat(heights, shape[position] // parts).reshape([-1 if axis == position else 1 for axis in range(len(shape))])
    return factor_of


def scatter_about(stream_key, shape, deviation, most, cuts=(), dtype=jnp.bfloat16):
    loudness = block_levels(stream_key, shape, cuts, -0.22, 0.18) if cuts else 1.0
    result = jax.random.normal(stream_key, shape, jnp.float32) * deviation * loudness
    return jnp.minimum(jnp.maximum(result, -most), most).astype(dtype)


def setup_inputs(seed: int = 0) -> dict:
    keys = jax.random.split(jax.random.key(seed), 8)
    return {
        "three_index": scatter_about(keys[0], (NAUX, NO, NB), 0.11, 0.69921875, ((0, 32),)),
        "virt_coeff": scatter_about(keys[1], (NB, NV), NB ** -0.5, 0.25),
        "metric_root": scatter_about(keys[2], (NAUX, NAUX), NAUX ** -0.5, 0.125, ((0, 32),)),
        "owner_table": jax.random.permutation(keys[3], NO).astype(jnp.int32),
        "pair_order": touch_ends(jax.random.randint(keys[4], (NSTEP,), 0, N_OCC), jax.random.fold_in(keys[4], 1), 0, N_OCC - 1).astype(jnp.int32),
        "occ_energy": jnp.clip(jax.random.uniform(keys[5], (NO,), jnp.float32, -1.5, -0.3), -1.5, -0.3),
        "vir_energy": jnp.clip(jax.random.uniform(keys[6], (NV,), jnp.float32, 0.1, 2.5), 0.1, 2.5),
    }


def reference(three_index, virt_coeff, metric_root, owner_table, pair_order, occ_energy, vir_energy):
    ordered = jnp.take(three_index, owner_table, axis=1)
    half = jnp.dot(ordered.reshape(NAUX * NO, NB), virt_coeff, preferred_element_type=jnp.float32)
    half = half.astype(jnp.bfloat16).reshape(NAUX, NO, NV)
    fitted = jnp.einsum("qp,pka->kaq", metric_root.astype(jnp.float32), half.astype(jnp.float32))
    fitted = fitted.astype(jnp.bfloat16)
    eps = occ_energy[owner_table]
    per_dev = NO // (N_OCC * N_VIR)
    block = NV // N_VIR
    density = jnp.zeros((NO, NV, NAUX), jnp.float32)
    for step in range(NSTEP):
        root = pair_order[step].astype(jnp.int32)
        pieces = []
        for vir_idx in range(N_VIR):
            start = ((root * N_VIR + vir_idx) * per_dev).astype(jnp.int32)
            partner = lax.dynamic_slice_in_dim(fitted, start, per_dev, 0).astype(jnp.float32)
            partner_eps = lax.dynamic_slice_in_dim(eps, start, per_dev, 0)
            own_rows = fitted[:, vir_idx * block:(vir_idx + 1) * block, :].astype(jnp.float32)
            block_eps = vir_energy[vir_idx * block:(vir_idx + 1) * block]
            pair = jnp.einsum("iaq,kbq->ikab", own_rows, partner)
            denom = (eps[:, None, None, None] + partner_eps[None, :, None, None]
                     - block_eps[None, None, :, None] - vir_energy[None, None, None, :])
            amp = (pair / denom).astype(jnp.bfloat16).astype(jnp.float32)
            pieces.append(jnp.einsum("ikab,kbq->iaq", amp, partner))
        density = density + jnp.concatenate(pieces, axis=1)
    return density
```

```python
import functools

import jax
import jax.numpy as jnp
from jax import lax
from jax.experimental import pallas as pl
from jax.experimental.pallas import tpu as pltpu
from jax.sharding import PartitionSpec as P

AXES = ("occ", "vir")
CHUNKS = 4
PARTS = 2
VMEM = 50 * 1024 * 1024


def half_body(x_ref, coeff_ref, perm_ref, out_ref):
    rows, orbitals, atomic = x_ref.shape
    half = jnp.dot(
        x_ref[...].reshape(rows * orbitals, atomic),
        coeff_ref[...],
        preferred_element_type=jnp.float32,
    ).astype(jnp.bfloat16)
    for row in range(rows):
        out_ref[row] = jnp.dot(
            perm_ref[...],
            half[row * orbitals : (row + 1) * orbitals],
            preferred_element_type=jnp.float32,
        ).astype(jnp.bfloat16)


def half_step(three_index, virt_coeff, perm):
    aux_rows, orbitals, atomic = three_index.shape
    virtuals = virt_coeff.shape[1]
    rows = min(8, aux_rows)
    return pl.pallas_call(
        half_body,
        grid=(aux_rows // rows,),
        in_specs=[
            pl.BlockSpec((rows, orbitals, atomic), lambda i: (i, 0, 0)),
            pl.BlockSpec((atomic, virtuals), lambda i: (0, 0)),
            pl.BlockSpec((orbitals, orbitals), lambda i: (0, 0)),
        ],
        out_specs=pl.BlockSpec((rows, orbitals, virtuals), lambda i: (i, 0, 0)),
        out_shape=jax.ShapeDtypeStruct((aux_rows, orbitals, virtuals), jnp.bfloat16),
        compiler_params=pltpu.CompilerParams(vmem_limit_bytes=VMEM),
        cost_estimate=pl.CostEstimate(
            flops=2 * aux_rows * orbitals * virtuals * (atomic + orbitals),
            bytes_accessed=2 * aux_rows * orbitals * (atomic + virtuals),
            transcendentals=0,
        ),
        name="half",
    )(three_index, virt_coeff, perm)


def pair_body(count, carried, own_ref, row_ref, cols_ref, *refs):
    partners = refs[:count]
    out_ref = refs[-1]

    @pl.when(pl.program_id(0) == 0)
    def _():
        out_ref[...] = refs[count][...] if carried else jnp.zeros_like(out_ref)

    for part, partner_ref in enumerate(partners):
        partner = partner_ref[...]
        pair = lax.dot_general(
            own_ref[...], partner, (((1,), (1,)), ((), ())), preferred_element_type=jnp.float32
        )
        amp = (pair / (row_ref[...] + cols_ref[part])).astype(jnp.bfloat16)
        out_ref[...] += jnp.dot(amp, partner, preferred_element_type=jnp.float32)


def pair_step(chunk, own, row, partners, cols, out, total, carried):
    rows, aux = own.shape
    count = partners[0].shape[0]
    width = min(512, count)
    in_specs = [
        pl.BlockSpec((rows, aux), lambda i: (0, 0)),
        pl.BlockSpec((rows, 1), lambda i: (0, 0)),
        pl.BlockSpec((len(partners), 1, width), lambda i: (0, 0, i)),
        *[pl.BlockSpec((width, aux), lambda i: (i, 0)) for _ in partners],
    ]
    operands = [own, row, jnp.stack(cols), *partners]
    aliases = {}
    if out is not None:
        in_specs.append(
            pl.BlockSpec((rows, aux), lambda i: (chunk, 0))
            if carried
            else pl.BlockSpec(memory_space=pl.ANY)
        )
        aliases = {len(operands): 0}
        operands.append(out)
    return pl.pallas_call(
        functools.partial(pair_body, len(partners), carried),
        grid=(count // width,),
        in_specs=in_specs,
        out_specs=pl.BlockSpec((rows, aux), lambda i: (chunk, 0)),
        out_shape=jax.ShapeDtypeStruct((total, aux), jnp.float32),
        input_output_aliases=aliases,
        compiler_params=pltpu.CompilerParams(vmem_limit_bytes=VMEM),
        cost_estimate=pl.CostEstimate(
            flops=4 * rows * count * len(partners) * aux,
            bytes_accessed=2 * count * len(partners) * aux + 6 * rows * aux,
            transcendentals=0,
        ),
        name="pair",
    )(*operands)


def over_chips(value):
    mine = gather_chips(value)
    return mine, swap_cores(mine)


def gather_chips(value):
    size = lax.axis_size("occ")
    groups = [list(range(core, size, 2)) for core in (0, 1)]
    return lax.all_gather(value, "occ", axis=0, tiled=True, axis_index_groups=groups)


def swap_cores(mine):
    size = lax.axis_size("occ")
    return lax.ppermute(mine, "occ", [(i, i + 1 - 2 * (i % 2)) for i in range(size)])


def gather_metric(metric_root):
    rows, aux = metric_root.shape
    column = lax.all_gather(metric_root, "vir", axis=0, tiled=True)
    mine, other = over_chips(column)
    shape = (lax.axis_size("occ") // 2, 1, column.shape[0], aux)
    mine, other = mine.reshape(shape), other.reshape(shape)
    even = lax.rem(lax.axis_index("occ"), 2) == 0
    both = jnp.concatenate(
        [jnp.where(even, mine, other), jnp.where(even, other, mine)], axis=1
    )
    return both.reshape(aux, aux)


def fit(metric, half):
    return jnp.einsum("pr,qp->rq", half, metric, preferred_element_type=jnp.float32).astype(
        jnp.bfloat16
    )


def local(three_index, virt_coeff, metric_root, owner_table, pair_order, occ_energy, vir_energy):
    aux_rows, orbitals, atomic = three_index.shape
    virtuals = virt_coeff.shape[1]
    occ_size = lax.axis_size("occ")
    vir_size = lax.axis_size("vir")
    devices = occ_size * vir_size
    per_dev = orbitals // devices
    group = orbitals // occ_size
    block = virtuals // vir_size
    steps = pair_order.shape[0]
    kept = group // CHUNKS
    per_part = steps // PARTS
    share = per_dev * virtuals // occ_size
    occ_idx = lax.axis_index("occ")
    vir_idx = lax.axis_index("vir")

    one_hot = owner_table[:, None] == jnp.arange(orbitals, dtype=jnp.int32)[None, :]
    eps = jnp.sum(jnp.where(one_hot, occ_energy[None, :], 0.0), axis=1)
    metric = gather_metric(metric_root)
    ordered = half_step(three_index, virt_coeff, one_hot.astype(jnp.bfloat16))

    def exchange(value):
        return lax.all_to_all(value, AXES, split_axis=0, concat_axis=0, tiled=True)

    def after(value, other):
        return lax.optimization_barrier((value, other))

    picked, cols = [], []
    for part in range(PARTS):
        roots = [pair_order[part * per_part + i] for i in range(per_part)]
        wanted = jnp.stack(
            [lax.dynamic_slice_in_dim(ordered, root * group, group, 1) for root in roots], axis=1
        )
        wanted = wanted.reshape(aux_rows, per_part, vir_size, occ_size, share)
        picked.append(wanted.transpose(3, 2, 0, 1, 4).reshape(devices, aux_rows, per_part * share))
        col = []
        for root in roots:
            start = (root * vir_size + vir_idx) * per_dev
            part_eps = lax.dynamic_slice_in_dim(eps, start, per_dev, 0)
            col.append((part_eps[:, None] - vir_energy[None, :]).reshape(occ_size, share))
        col = jnp.stack(col, axis=1).reshape(occ_size // 2, 2, per_part * share)
        core = lax.rem(occ_idx, 2)
        cols.append([jnp.take(col, c, axis=1).reshape(1, -1) for c in (core, 1 - core)])

    own_eps = lax.dynamic_slice_in_dim(eps, occ_idx * group, group, 0)
    block_eps = lax.dynamic_slice_in_dim(vir_energy, vir_idx * block, block, 0)
    row = (own_eps[:, None] - block_eps[None, :]).reshape(CHUNKS, kept * block, 1)
    split = ordered.reshape(aux_rows, occ_size, CHUNKS, kept, vir_size, block)
    split = [
        split[:, :, chunk].transpose(1, 3, 0, 2, 4).reshape(devices, aux_rows, kept * block)
        for chunk in range(CHUNKS)
    ]

    def partner_of(taken):
        mine = fit(metric, taken.reshape(devices * aux_rows, per_part * share))
        return mine, gather_chips(mine)

    def own_of(owned):
        return fit(metric, owned.reshape(devices * aux_rows, kept * block))

    total = group * block
    taken, split, picked[1] = lax.optimization_barrier((exchange(picked[0]), split, picked[1]))
    mine, first = partner_of(taken)
    owned, mine = after(exchange(split[0]), mine)
    own = own_of(owned)
    taken, own = after(exchange(picked[1]), own)
    mine, second = partner_of(taken)
    first = [first, swap_cores(first)]
    out, owns = None, [own]
    early = CHUNKS - 1
    for chunk in range(early):
        if chunk:
            owned, out = after(exchange(split[chunk]), out)
            if chunk == early - 1:
                second, out = after(second, out)
                second = [second, swap_cores(second)]
            owns.append(own_of(owned))
        out = pair_step(chunk, owns[chunk], row[chunk], first, cols[0], out, total, False)
    for chunk in range(early):
        out = pair_step(chunk, owns[chunk], row[chunk], second, cols[1], out, total, True)
    owned, out = after(exchange(split[early]), out)
    own = own_of(owned)
    both = [*first, *second]
    out = pair_step(early, own, row[early], both, [*cols[0], *cols[1]], out, total, False)
    return out.reshape(group, block, out.shape[1])


def solution(mesh):
    placed = (P(AXES, None, None), P(), P(AXES, None), P(), P(), P(), P())
    return jax.shard_map(
        local, mesh=mesh, in_specs=placed, out_specs=P("occ", "vir", None), check_vma=False
    )
```
